512 devices in a mesh: dp: 64 (over y, x, core), mp: 8 (over z).
Axes of the slice: x: 4, y: 8, z: 8, core: 2. Of those that a mesh axis runs over, the one named last changes fastest.
Arguments:
- activations: bfloat16 [32768, 8192], P('dp', 'mp'), may hold values from -16 to 16
- cotangent: bfloat16 [32768, 8192], P('dp', 'mp'), may hold values from -0.099121094 to 0.099121094
- basis: bfloat16 [8192, 1024], P('mp'), may hold values from -0.0625 to 0.0625
- weight: bfloat16 [8192, 8192], P(('mp', 'dp')), may hold values from -3 to 3
- first_moment: float32 [8192, 1024], P(('mp', 'dp')), may hold values from -3 to 3
- second_moment: float32 [8192, 1024], P(('mp', 'dp')), may hold values from 0.05 to 2
Outputs:
- new_weight: bfloat16 [8192, 8192], P(('mp', 'dp'))
- new_first: float32 [8192, 1024], P(('mp', 'dp'))
- new_second: float32 [8192, 1024], P(('mp', 'dp'))
The draws below stay inside these ranges and needn't reach their ends.
All inputs are finite; a program needn't handle non-finite values.
Results may differ from the reference program's by a relative error of at most 0.002.
Values may be sent and summed in bfloat16 or wider, within the bound.
A program may use at most 64 MiB of HBM per device.

```python
import math
import jax
import jax.numpy as jnp
from jax import lax

D = 8192
RANK = 1024
STEP = 1000
TOKENS = 32768


def spiked(values, stream_key, source, target, blocks, factor):
    owner, partner = [(jnp.arange(values.shape[position]) // (values.shape[position] // blocks)).reshape([-1 if axis == position else 1 for axis in range(values.ndim)]) for position in (source, target)]
    chosen = jax.random.permutation(stream_key, blocks)[partner]
    strong = (owner == chosen) | (owner == (partner + blocks // 2) % blocks)
    return jnp.where(strong, factor * values, values)


def levels(rng, shape, split, smallest, largest):
    factor_of, own = 1.0, jax.random.fold_in(rng, 6)
    for axis_at, blocks in split:
        steps = jnp.exp(jax.random.uniform(jax.random.fold_in(own, axis_at), (blocks,), jnp.float32, smallest / len(split), largest / len(split)))
        factor_of = factor_of * jnp.repeat(steps, shape[axis_at] // blocks).reshape([-1 if axis == axis_at else 1 for axis in range(len(shape))])
    return factor_of


def bell_draw(own_key, dims, scale, limit, shards=(), dtype=jnp.bfloat16):
    loudness = levels(own_key, dims, shards, -0.22, 0.18) if shards else 1.0
    values = jax.random.normal(own_key, dims, jnp.float32) * scale * loudness
    return jnp.minimum(jnp.maximum(values, -limit), limit).astype(dtype)


def bell_draw_with(own_key, dims, spread, bound, split, heavy, kind=jnp.bfloat16):
    values = spread * jax.random.normal(own_key, dims, jnp.float32)
    if split:
        values = values * levels(own_key, dims, split, -0.22, 0.18)
    return jnp.clip(spiked(values, jax.random.fold_in(own_key, 3), *heavy), -bound, bound).astype(kind)


def setup_inputs(seed: int = 0) -> dict:
    key_list = jax.random.split(jax.random.key(seed), 7)
    activations = bell_draw_with(key_list[0], (TOKENS, D), 1.0, 16.0, ((0, 64), (1, 8)), (0, 1, 64, 4.0))
    cotangent = bell_draw(key_list[1], (TOKENS, D), (3.0 / (TOKENS ** 0.5)), 0.099121094, ((0, 64), (1, 8)))
    basis = bell_draw(key_list[2], (D, RANK), D ** -0.5, 0.0625, ((0, 8),))
    weight = bell_draw(key_list[3], (D, D), 0.5, 3.0, ((0, 512),))
    first_moment = bell_draw(key_list[4], (D, RANK), 0.5, 3.0, ((0, 512),), jnp.float32)
    second_moment = jnp.clip(jnp.exp(math.log(2.0) - 3.6888794 * jax.random.uniform(key_list[5], (D, RANK), jnp.float32) ** levels(key_list[5], (D, RANK), ((0, 512),), -0.2, 0.2)), 0.05, 2.0)
    return dict(activations=activations, cotangent=cotangent, basis=basis, weight=weight, first_moment=first_moment, second_moment=second_moment)


beta_first = 0.9
beta_second = 0.999
adam_eps = 1e-08
step_rate = 0.1

def reference(activations, cotangent, basis, weight, first_moment, second_moment):
    projected = jnp.dot(cotangent, basis, preferred_element_type=jnp.float32).astype(jnp.bfloat16)
    grad = lax.dot_general(activations, projected, (((0,), (0,)), ((), ())), preferred_element_type=jnp.float32)
    new_first = beta_first * first_moment + (1.0 - beta_first) * grad
    new_second = beta_second * second_moment + (1.0 - beta_second) * grad * grad
    first_hat = new_first / (1.0 - beta_first ** STEP)
    second_hat = new_second / (1.0 - beta_second ** STEP)
    low_rank = (first_hat / (jnp.sqrt(second_hat) + adam_eps)).astype(jnp.bfloat16)
    delta = lax.dot_general(low_rank, basis, (((1,), (1,)), ((), ())), preferred_element_type=jnp.float32).astype(jnp.bfloat16)
    new_weight = (weight.astype(jnp.float32) - step_rate * delta.astype(jnp.float32)).astype(jnp.bfloat16)
    return (new_weight, new_first, new_second)
```

```python
import jax
import jax.numpy as jnp
from jax import lax
from jax.experimental import pallas as pl
from jax.experimental.pallas import tpu as pltpu
from jax.sharding import PartitionSpec as P

STEP = 1000

beta_first = 0.9
beta_second = 0.999
adam_eps = 1e-08
step_rate = 0.1

MESH = pl.DeviceIdType.MESH
F32, BF16 = jnp.float32, jnp.bfloat16

PARENT = {4: 3, 3: 1, 2: 1, 1: 0, -3: -2, -2: -1, -1: 0}
SLOT = {o: i for i, o in enumerate(PARENT)}
CHUNKS = 4
WIDTH = 1024 // CHUNKS
LIFT = 2.0**24


def children(node):
    return [o for o in PARENT if PARENT[o] == node]


def height(node):
    return 1 + max([height(o) for o in children(node)], default=-1)


def depth(node):
    return 0 if node == 0 else 1 + depth(PARENT[node])


def encode(value):
    return ((value * value) * (value * jnp.abs(value))).astype(BF16)


def decode(code):
    code = code.astype(F32)
    root = lax.rsqrt(jnp.maximum(jnp.abs(code), 1e-37))
    return code * (root * root) * lax.rsqrt(root)


def each(function):
    lax.fori_loop(0, CHUNKS, lambda c, carry: (function(c), carry)[1], 0)


def kernel(
    act_in, cot_in, basis_in, weight_in, first_in, second_in,
    weight_out, first_out, second_out,
    act, cot, basis, weight, first, second,
    partial, rs_send, rs_recv, proj, act_t, own, core_send, core_recv,
    x_send, x_recv, y_sum, y_send, y_recv, low, total, d_send, d_recv,
    load_sem, rs_ss, rs_rs, ag_ss, ag_rs, core_ss, core_rs, x_ss, x_rs, y_ss, y_rs, low_ss, low_rs, d_ss, d_rs,
):
    dp, z = lax.axis_index("dp"), lax.axis_index("mp")
    y, x, core = dp // 8, (dp // 2) % 4, dp % 2
    sign = 1 - 2 * core

    def along_z(offset):
        return lax.rem(z + sign * offset + 16, 8)

    def at(y_to, x_to, core_to, z_to):
        return ((y_to * 4 + x_to) * 2 + core_to, z_to)

    def z_peer(offset):
        return at(y, x, core, along_z(offset))

    def x_peer(k):
        return at(y, lax.rem(x + k, 4), core, z)

    def y_peer(k):
        return at(lax.rem(y + k, 8), x, core, z)

    core_peer = at(y, x, 1 - core, z)

    def columns(c):
        return pl.ds(pl.multiple_of(c * WIDTH, WIDTH), WIDTH)

    def load(i, source, target):
        return pltpu.make_async_copy(source, target, load_sem.at[i])

    cot_load = load(0, cot_in, cot)
    act_load = load(1, act_in, act)
    weight_load = load(2, weight_in, weight)
    first_load = load(3, first_in, first)
    second_load = load(4, second_in, second)

    def basis_load(c):
        return load(5 + c, basis_in.at[:, columns(c)], basis.at[c])

    cot_load.start()
    each(lambda c: basis_load(c).start())
    act_load.start()
    first_load.start()
    second_load.start()
    weight_load.start()

    barrier = pltpu.get_barrier_semaphore()
    peers = [z_peer(k) for k in range(1, 8)] + [x_peer(k) for k in range(1, 4)]
    peers += [y_peer(k) for k in range(1, 8)] + [core_peer]
    for peer in peers:
        pl.semaphore_signal(barrier, inc=1, device_id=peer, device_id_type=MESH)

    def send(source, target, send_sem, recv_sem, peer):
        return pltpu.make_async_remote_copy(
            src_ref=source,
            dst_ref=target,
            send_sem=send_sem,
            recv_sem=recv_sem,
            device_id=peer,
            device_id_type=MESH,
        )

    def rs_copy(c, o):
        i = SLOT[o]
        return send(rs_send.at[c, i], rs_recv.at[c, i], rs_ss.at[c, i], rs_rs.at[c, i], z_peer(PARENT[o] - o))

    def ag_copy(c, o):
        i, block = SLOT[o], along_z(-PARENT[o])
        return send(
            proj.at[c, block], proj.at[c, block], ag_ss.at[c, i], ag_rs.at[c, i], z_peer(o - PARENT[o])
        )

    def core_copy(c):
        return send(core_send.at[c], core_recv.at[c], core_ss.at[c], core_rs.at[c], core_peer)

    def x_copy(c, k):
        return send(x_send.at[c, k - 1], x_recv.at[c, k - 1], x_ss.at[c, k - 1], x_rs.at[c, k - 1], x_peer(k))

    def y_copy(c, k):
        return send(y_send.at[c, k - 1], y_recv.at[c, k - 1], y_ss.at[c, k - 1], y_rs.at[c, k - 1], y_peer(k))

    def low_copy(c, k):
        return send(low.at[c, z], low.at[c, z], low_ss.at[c, k - 1], low_rs.at[c, k - 1], z_peer(k))

    def d_copy(k):
        return send(d_send.at[along_z(k)], d_recv.at[k - 1], d_ss.at[k - 1], d_rs.at[k - 1], z_peer(k))

    def rs_step(c, o):
        value = partial[c, along_z(-o)]
        for child in children(o):
            rs_copy(c, child).wait_recv()
            value += decode(rs_recv[c, SLOT[child]])
        rs_send[c, SLOT[o]] = encode(value)
        rs_copy(c, o).start()

    cot_load.wait()

    def multiply(c):
        basis_load(c).wait()
        product = jnp.dot(cot[...], basis[c], preferred_element_type=F32)
        partial[c] = (product * LIFT).reshape(8, 64, WIDTH)

    multiply(0)
    pl.semaphore_wait(barrier, len(peers))

    def first_sends(c):
        @pl.when(c > 0)
        def _():
            multiply(c)

        for o in PARENT:
            if height(o) == 0:
                rs_step(c, o)

    each(first_sends)

    act_load.wait()

    def transpose(i):
        block = act[:, pl.ds(pl.multiple_of(i * 128, 128), 128)].T.reshape(4, 2, 16, 512)
        for j in range(4):
            for k in range(2):
                act_t[k, j, i] = block[j, k]

    lax.fori_loop(0, 8, lambda i, carry: (transpose(i), carry)[1], 0)

    for level in range(1, height(0)):

        def later_sends(c):
            for o in PARENT:
                if height(o) == level:
                    rs_step(c, o)

        each(later_sends)

    def own_block(c):
        value = partial[c, z]
        for child in children(0):
            rs_copy(c, child).wait_recv()
            value += decode(rs_recv[c, SLOT[child]])
        proj[c, z] = (value * (1.0 / LIFT)).astype(BF16)
        for o in children(0):
            ag_copy(c, o).start()

    each(own_block)

    def received(c, o):
        ag_copy(c, o).wait_recv()

    for level in range(1, 1 + max(depth(o) for o in PARENT)):

        def forward(c):
            for o in PARENT:
                if depth(o) == level:
                    received(c, o)
                    for child in children(o):
                        ag_copy(c, child).start()

        each(forward)

    def gradient(c):
        here = proj[c].reshape(512, WIDTH)
        core_send[c] = jnp.dot(act_t[1 - core].reshape(512, 512), here, preferred_element_type=F32).reshape(4, 128, WIDTH)
        core_copy(c).start()
        own[c] = jnp.dot(act_t[core].reshape(512, 512), here, preferred_element_type=F32).reshape(4, 128, WIDTH)

    each(gradient)

    def over_x(c):
        core_copy(c).wait_recv()
        for k in (2, 1, 3):
            to = lax.rem(x + k, 4)
            x_send[c, k - 1] = encode(own[c, to] + core_recv[c, to])
            x_copy(c, k).start()

    each(over_x)

    def over_y(c):
        value = own[c, x] + core_recv[c, x]
        for k in range(1, 4):
            x_copy(c, k).wait_recv()
            value += decode(x_recv[c, k - 1])
        y_sum[c] = value.reshape(8, 16, WIDTH)
        for k in (4, 3, 5, 2, 6, 1, 7):
            y_send[c, k - 1] = encode(y_sum[c, lax.rem(y + k, 8)])
            y_copy(c, k).start()

    each(over_y)

    first_load.wait()
    second_load.wait()

    def adam(c):
        grad = y_sum[c, y]
        for k in range(1, 8):
            y_copy(c, k).wait_recv()
            grad += decode(y_recv[c, k - 1])
        new_first = beta_first * first[:, columns(c)] + (1.0 - beta_first) * grad
        new_second = beta_second * second[:, columns(c)] + (1.0 - beta_second) * grad * grad
        first_out[:, columns(c)] = new_first
        second_out[:, columns(c)] = new_second
        first_hat = new_first / (1.0 - beta_first**STEP)
        second_hat = new_second / (1.0 - beta_second**STEP)
        low[c, z] = (first_hat / (jnp.sqrt(second_hat) + adam_eps)).astype(BF16)
        for k in (4, 3, 5, 2, 6, 1, 7):
            low_copy(c, k).start()

    each(adam)

    total[...] = jnp.zeros_like(total)

    def expand(c):
        for k in range(1, 8):
            low_copy(c, k).wait_recv()
        total[...] += lax.dot_general(
            low[c].reshape(128, WIDTH), basis[c], (((1,), (1,)), ((), ())), preferred_element_type=F32
        )

    each(expand)
    d_send[...] = total[...].astype(BF16).reshape(8, 16, 1024)
    for k in (4, 3, 5, 2, 6, 1, 7):
        d_copy(k).start()

    weight_load.wait()

    def update(block, delta):
        place = pl.ds(pl.multiple_of(block * 1024, 1024), 1024)
        value = weight[:, place].astype(F32) - step_rate * delta.astype(F32)
        weight_out[:, place] = value.astype(BF16)

    update(z, d_send[z])
    for k in (1, 7, 2, 6, 3, 5, 4):
        d_copy(k).wait_recv()
        update(along_z(-k), d_recv[k - 1])

    def drain(c):
        for o in PARENT:
            rs_copy(c, o).wait_send()
            ag_copy(c, o).wait_send()
        core_copy(c).wait_send()
        for k in range(1, 4):
            x_copy(c, k).wait_send()
        for k in range(1, 8):
            y_copy(c, k).wait_send()
            low_copy(c, k).wait_send()

    each(drain)
    for k in range(1, 8):
        d_copy(k).wait_send()


def body(activations, cotangent, basis, weight, first_moment, second_moment):
    vmem, dma = pltpu.VMEM, pltpu.SemaphoreType.DMA
    return pl.pallas_call(
        kernel,
        out_shape=(
            jax.ShapeDtypeStruct((16, 8192), BF16),
            jax.ShapeDtypeStruct((16, 1024), F32),
            jax.ShapeDtypeStruct((16, 1024), F32),
        ),
        in_specs=[pl.BlockSpec(memory_space=pl.ANY)] * 6,
        out_specs=(pl.BlockSpec(memory_space=pltpu.VMEM),) * 3,
        scratch_shapes=[
            vmem((512, 1024), BF16),
            vmem((512, 1024), BF16),
            vmem((CHUNKS, 1024, WIDTH), BF16),
            vmem((16, 8192), BF16),
            vmem((16, 1024), F32),
            vmem((16, 1024), F32),
            vmem((CHUNKS, 8, 64, WIDTH), F32),
            vmem((CHUNKS, 7, 64, WIDTH), BF16),
            vmem((CHUNKS, 7, 64, WIDTH), BF16),
            vmem((CHUNKS, 8, 64, WIDTH), BF16),
            vmem((2, 4, 8, 16, 512), BF16),
            vmem((CHUNKS, 4, 128, WIDTH), F32),
            vmem((CHUNKS, 4, 128, WIDTH), F32),
            vmem((CHUNKS, 4, 128, WIDTH), F32),
            vmem((CHUNKS, 3, 128, WIDTH), BF16),
            vmem((CHUNKS, 3, 128, WIDTH), BF16),
            vmem((CHUNKS, 8, 16, WIDTH), F32),
            vmem((CHUNKS, 7, 16, WIDTH), BF16),
            vmem((CHUNKS, 7, 16, WIDTH), BF16),
            vmem((CHUNKS, 8, 16, WIDTH), BF16),
            vmem((128, 1024), F32),
            vmem((8, 16, 1024), BF16),
            vmem((7, 16, 1024), BF16),
            dma((5 + CHUNKS,)),
            dma((CHUNKS, 7)),
            dma((CHUNKS, 7)),
            dma((CHUNKS, 7)),
            dma((CHUNKS, 7)),
            dma((CHUNKS,)),
            dma((CHUNKS,)),
            dma((CHUNKS, 3)),
            dma((CHUNKS, 3)),
            dma((CHUNKS, 7)),
            dma((CHUNKS, 7)),
            dma((CHUNKS, 7)),
            dma((CHUNKS, 7)),
            dma((7,)),
            dma((7,)),
        ],
        compiler_params=pltpu.CompilerParams(
            collective_id=1, has_side_effects=True, vmem_limit_bytes=48 * 2**20
        ),
        name="galore_step",
    )(activations, cotangent, basis, weight, first_moment, second_moment)


def solution(mesh):
    rows = P(("mp", "dp"), None)
    return jax.shard_map(
        body,
        mesh=mesh,
        in_specs=(P("dp", "mp"), P("dp", "mp"), P("mp", None), rows, rows, rows),
        out_specs=(rows, rows, rows),
        check_vma=False,
    )
```

```python
import functools

import jax
import jax.numpy as jnp
from jax import lax
from jax.experimental import pallas as pl
from jax.experimental.pallas import tpu as pltpu
from jax.sharding import PartitionSpec as P

STEP = 1000

beta_first = 0.9
beta_second = 0.999
adam_eps = 1e-08
step_rate = 0.1

MESH = pl.DeviceIdType.MESH
F32, BF16 = jnp.float32, jnp.bfloat16

TREES = (
    {4: 2, 3: 2, 2: 0, 1: 0, -3: -2, -2: 0, -1: 0},
    {4: 3, 3: 2, 2: 1, 1: 0, -3: -2, -2: -1, -1: 0},
)
SLOT = {o: i for i, o in enumerate((3, 1, -3, -1, 4, 2, -2))}
JOINED = (((3, 1), (-3, -1)), ())
CHUNKS = 4
AHEAD = 1
GROUPS = 4
EACH = CHUNKS // GROUPS
WIDTH = 1024 // CHUNKS
WIDE = 1024 // GROUPS
LIFT = 2.0**24


def children(tree, node):
    return [o for o in tree if tree[o] == node]


def height(tree, node):
    return 1 + max([height(tree, o) for o in children(tree, node)], default=-1)


def depth(tree, node):
    return 0 if node == 0 else 1 + depth(tree, tree[node])


def encode(value):
    return ((value * value) * (value * jnp.abs(value))).astype(BF16)


def decode(code):
    code = code.astype(F32)
    root = lax.rsqrt(jnp.maximum(jnp.abs(code), 1e-37))
    return code * (root * root) * lax.rsqrt(root)


def each(function, count=CHUNKS):
    lax.fori_loop(0, count, lambda c, carry: (function(c), carry)[1], 0)


def kernel(
    act_in, cot_in, basis_in, weight_in, first_in, second_in,
    weight_out, first_out, second_out,
    act, cot, basis, weight, first, second,
    partial, rs_send, rs_recv, proj, act_t, own, core_send, core_recv,
    x_send, x_recv, y_sum, y_send, y_recv, low, total, d_send, d_recv,
    load_sem, rs_ss, rs_rs, ag_ss, ag_rs, core_ss, core_rs, x_ss, x_rs, y_ss, y_rs, low_ss, low_rs, d_ss, d_rs,
    near_sem, far_sem,
):
    dp, z = lax.axis_index("dp"), lax.axis_index("mp")
    y, x, core = dp // 8, (dp // 2) % 4, dp % 2
    sign = 1 - 2 * core

    def along_z(offset):
        return lax.rem(z + sign * offset + 16, 8)

    def at(y_to, x_to, core_to, z_to):
        return ((y_to * 4 + x_to) * 2 + core_to, z_to)

    def z_peer(offset):
        return at(y, x, core, along_z(offset))

    def x_peer(k):
        return at(y, lax.rem(x + k, 4), core, z)

    def y_peer(k):
        return at(lax.rem(y + k, 8), x, core, z)

    core_peer = at(y, x, 1 - core, z)

    def columns(c):
        return pl.ds(pl.multiple_of(c * WIDTH, WIDTH), WIDTH)

    barrier = pltpu.get_barrier_semaphore()
    peers = [z_peer(k) for k in (1, -1, 2, -2)] + [core_peer] + [x_peer(k) for k in (1, 3, 2)]
    peers += [y_peer(k) for k in (1, 7)]
    for peer in peers:
        pl.semaphore_signal(barrier, inc=1, device_id=peer, device_id_type=MESH)

    def wide(g):
        return pl.ds(pl.multiple_of(g * WIDE, WIDE), WIDE)

    def load(i, source, target):
        return pltpu.make_async_copy(source, target, load_sem.at[i])

    cot_load = load(0, cot_in, cot)
    act_load = load(1, act_in, act)
    weight_load = load(2, weight_in, weight)
    first_load = load(3, first_in, first)
    second_load = load(4, second_in, second)

    def basis_load(c):
        return load(5 + c, basis_in.at[:, columns(c)], basis.at[c])

    cot_load.start()
    each(lambda c: basis_load(c).start())
    act_load.start()
    first_load.start()
    second_load.start()
    weight_load.start()

    def send(source, target, send_sem, recv_sem, peer):
        return pltpu.make_async_remote_copy(
            src_ref=source,
            dst_ref=target,
            send_sem=send_sem,
            recv_sem=recv_sem,
            device_id=peer,
            device_id_type=MESH,
        )

    def rs_copy(tree, c, o, size=1):
        i = SLOT[o]
        place = pl.ds(i, size)
        return send(
            rs_send.at[c, place], rs_recv.at[c, place], rs_ss.at[c, i], rs_rs.at[c, i], z_peer(tree[o] - o)
        )

    def ag_copy(tree, c, o):
        i, block = SLOT[o], along_z(-tree[o])
        return send(proj.at[c, block], proj.at[c, block], ag_ss.at[c, i], ag_rs.at[c, i], z_peer(o - tree[o]))

    def core_copy(c):
        return send(core_send.at[c], core_recv.at[c], core_ss.at[c], core_rs.at[c], core_peer)

    def x_copy(c, k):
        return send(x_send.at[c, k - 1], x_recv.at[c, k - 1], x_ss.at[c], x_rs.at[c], x_peer(k))

    def x_all(c):
        return send(x_send.at[c], x_recv.at[c], x_ss.at[c], x_rs.at[c], x_peer(1))

    def y_copy(g, k):
        return send(y_send.at[g, k - 1], y_recv.at[g, k - 1], y_ss.at[g], y_rs.at[g], y_peer(k))

    def y_all(g):
        return send(y_send.at[g], y_recv.at[g], y_ss.at[g], y_rs.at[g], y_peer(1))

    def low_copy(g, k):
        return send(low.at[g, z], low.at[g, z], low_ss.at[g], low_rs.at[g], z_peer(k))

    def low_all(g):
        seven = low.at[g, pl.ds(0, 7)]
        return send(seven, seven, low_ss.at[g], low_rs.at[g], z_peer(1))

    def d_copy(k):
        return send(d_send.at[along_z(k)], d_recv.at[k - 1], d_ss.at[k - 1], d_rs.at[k - 1], z_peer(k))

    def multiply(c):
        basis_load(c).wait()
        product = jnp.dot(cot[...], basis[c], preferred_element_type=F32)
        partial[c] = (product * LIFT).reshape(8, 64, WIDTH)

    def meet(semaphore, distance):
        for k in (distance, 8 - distance):
            pl.semaphore_signal(semaphore, inc=1, device_id=y_peer(k), device_id_type=MESH)
        pl.semaphore_wait(semaphore, 2)

    def transpose(i):
        block = act[:, pl.ds(pl.multiple_of(i * 128, 128), 128)].T.reshape(4, 2, 16, 512)
        for j in range(4):
            for k in range(2):
                act_t[k, j, i] = block[j, k]

    def project(tree, joined):
        size = {o: 1 for o in tree} | {pair[0]: 2 for pair in joined}
        second = {pair[1]: pair[0] for pair in joined}
        seen = set()

        def arrived(c, o):
            first = second.get(o, o)
            if first not in seen:
                rs_copy(tree, c, first, size[first]).wait_recv()
            return decode(rs_recv[c, SLOT[o]])

        def note(nodes):
            seen.update(second.get(o, o) for o in nodes)

        def rs_step(c, o):
            value = partial[c, along_z(-o)]
            for child in children(tree, o):
                value += arrived(c, child)
            rs_send[c, SLOT[o]] = encode(value)

        def rs_start(c, o):
            if o not in second:
                rs_copy(tree, c, o, size[o]).start()

        def first_sends(c):
            @pl.when(c > 0)
            def _():
                multiply(c)

            for o in [o for o in tree if height(tree, o) == 0]:
                rs_step(c, o)
                if size[o] == 1 and o not in second:
                    rs_copy(tree, c, o).start()
                elif o in second:
                    rs_copy(tree, c, second[o], 2).start()

        each(first_sends)
        act_load.wait()
        lax.fori_loop(0, 8, lambda i, carry: (transpose(i), carry)[1], 0)
        meet(near_sem, 1)

        for level in range(1, height(tree, 0)):

            nodes = [o for o in tree if height(tree, o) == level]

            def later_sends(c):
                for o in nodes:
                    rs_step(c, o)
                    rs_start(c, o)

            each(later_sends)
            note(child for o in nodes for child in children(tree, o))

        meet(far_sem, 2)

        def own_block(c):
            value = partial[c, z]
            for child in children(tree, 0):
                value += arrived(c, child)
            proj[c, z] = (value * (1.0 / LIFT)).astype(BF16)
            for o in children(tree, 0):
                ag_copy(tree, c, o).start()

        each(own_block)

        for level in range(1, max(depth(tree, o) for o in tree)):

            def forward(c):
                for o in tree:
                    if depth(tree, o) == level and children(tree, o):
                        ag_copy(tree, c, o).wait_recv()
                        for child in children(tree, o):
                            ag_copy(tree, c, child).start()

            each(forward)

    def wait_leaves(tree, c):
        for o in tree:
            if not children(tree, o):
                ag_copy(tree, c, o).wait_recv()

    cot_load.wait()
    multiply(0)
    pl.semaphore_wait(barrier, len(peers))

    for number, tree in enumerate(TREES):
        pl.when(core == number)(functools.partial(project, tree, JOINED[number]))

    def gradient(c):
        for number, tree in enumerate(TREES):
            pl.when(core == number)(functools.partial(wait_leaves, tree, c))
        here = proj[c].reshape(512, WIDTH)
        other = jnp.dot(act_t[1 - core].reshape(512, 512), here, preferred_element_type=F32)
        core_send[c] = other.reshape(4, 128, WIDTH)
        core_copy(c).start()
        mine = jnp.dot(act_t[core].reshape(512, 512), here, preferred_element_type=F32)
        own[c] = mine.reshape(4, 128, WIDTH)

    def over_x(c):
        core_copy(c).wait_recv()
        for k in (2, 1, 3):
            to = lax.rem(x + k, 4)
            x_send[c, k - 1] = encode(own[c, to] + core_recv[c, to])
            x_copy(c, k).start()

    def gradient_and_x(c):
        over_x(c)

        @pl.when(c + AHEAD < CHUNKS)
        def _():
            gradient(c + AHEAD)

    for c in range(AHEAD):
        gradient(c)
    each(gradient_and_x)

    def over_y(g):
        for j in range(EACH):
            c = g * EACH + j
            value = own[c, x] + core_recv[c, x]
            x_all(c).wait_recv()
            for k in range(1, 4):
                value += decode(x_recv[c, k - 1])
            y_sum[g, :, :, j * WIDTH : (j + 1) * WIDTH] = value.reshape(8, 16, WIDTH)
        for k in (4, 3, 5, 2, 6, 1, 7):
            y_send[g, k - 1] = encode(y_sum[g, lax.rem(y + k, 8)])
            y_copy(g, k).start()

    each(over_y, GROUPS)

    first_load.wait()
    second_load.wait()

    def adam(g):
        grad = y_sum[g, y]
        y_all(g).wait_recv()
        for k in range(1, 8):
            grad += decode(y_recv[g, k - 1])
        new_first = beta_first * first[:, wide(g)] + (1.0 - beta_first) * grad
        new_second = beta_second * second[:, wide(g)] + (1.0 - beta_second) * grad * grad
        first_out[:, wide(g)] = new_first
        second_out[:, wide(g)] = new_second
        first_hat = new_first / (1.0 - beta_first**STEP)
        second_hat = new_second / (1.0 - beta_second**STEP)
        low[g, z] = (first_hat / (jnp.sqrt(second_hat) + adam_eps)).astype(BF16)
        for k in (4, 3, 5, 2, 6, 1, 7):
            low_copy(g, k).start()

    each(adam, GROUPS)

    total[...] = jnp.zeros_like(total)

    def expand(g):
        low_all(g).wait_recv()
        for j in range(EACH):
            total[...] += lax.dot_general(
                low[g, :, :, j * WIDTH : (j + 1) * WIDTH].reshape(128, WIDTH),
                basis[g * EACH + j],
                (((1,), (1,)), ((), ())),
                preferred_element_type=F32,
            )

    each(expand, GROUPS)
    d_send[...] = total[...].astype(BF16).reshape(8, 16, 1024)
    for k in (4, 3, 5, 2, 6, 1, 7):
        d_copy(k).start()

    def drain_z(tree, joined, c):
        size = {o: 1 for o in tree} | {pair[0]: 2 for pair in joined} | {pair[1]: 0 for pair in joined}
        for o in tree:
            if size[o]:
                rs_copy(tree, c, o, size[o]).wait_send()
            ag_copy(tree, c, o).wait_send()

    def drain(c):
        for number, tree in enumerate(TREES):
            pl.when(core == number)(functools.partial(drain_z, tree, JOINED[number], c))
        core_copy(c).wait_send()
        x_all(c).wait_send()

    def drain_group(g):
        y_all(g).wait_send()
        low_all(g).wait_send()

    each(drain)
    each(drain_group, GROUPS)

    weight_load.wait()

    def update(block, delta):
        place = pl.ds(pl.multiple_of(block * 1024, 1024), 1024)
        value = weight[:, place].astype(F32) - step_rate * delta.astype(F32)
        weight_out[:, place] = value.astype(BF16)

    update(z, d_send[z])
    for k in (1, 7, 2, 6, 3, 5, 4):
        d_copy(k).wait_recv()
        update(along_z(-k), d_recv[k - 1])
    for k in range(1, 8):
        d_copy(k).wait_send()


def store(weight, first, second, weight_out, first_out, second_out, sem):
    copies = [
        pltpu.make_async_copy(source, target, sem.at[i])
        for i, (source, target) in enumerate(((weight, weight_out), (first, first_out), (second, second_out)))
    ]
    for copy in copies:
        copy.start()
    for copy in copies:
        copy.wait()


def body(activations, cotangent, basis, weight, first_moment, second_moment):
    vmem, dma = pltpu.VMEM, pltpu.SemaphoreType.DMA
    results = pl.pallas_call(
        kernel,
        out_shape=(vmem((16, 8192), BF16), vmem((16, 1024), F32), vmem((16, 1024), F32)),
        in_specs=[pl.BlockSpec(memory_space=pltpu.HBM)] * 6,
        out_specs=(pl.BlockSpec(memory_space=pltpu.VMEM),) * 3,
        scratch_shapes=[
            vmem((512, 1024), BF16),
            vmem((512, 1024), BF16),
            vmem((CHUNKS, 1024, WIDTH), BF16),
            vmem((16, 8192), BF16),
            vmem((16, 1024), F32),
            vmem((16, 1024), F32),
            vmem((CHUNKS, 8, 64, WIDTH), F32),
            vmem((CHUNKS, 7, 64, WIDTH), BF16),
            vmem((CHUNKS, 7, 64, WIDTH), BF16),
            vmem((CHUNKS, 8, 64, WIDTH), BF16),
            vmem((2, 4, 8, 16, 512), BF16),
            vmem((CHUNKS, 4, 128, WIDTH), F32),
            vmem((CHUNKS, 4, 128, WIDTH), F32),
            vmem((CHUNKS, 4, 128, WIDTH), F32),
            vmem((CHUNKS, 3, 128, WIDTH), BF16),
            vmem((CHUNKS, 3, 128, WIDTH), BF16),
            vmem((GROUPS, 8, 16, WIDE), F32),
            vmem((GROUPS, 7, 16, WIDE), BF16),
            vmem((GROUPS, 7, 16, WIDE), BF16),
            vmem((GROUPS, 8, 16, WIDE), BF16),
            vmem((128, 1024), F32),
            vmem((8, 16, 1024), BF16),
            vmem((7, 16, 1024), BF16),
            dma((5 + CHUNKS,)),
            dma((CHUNKS, 7)),
            dma((CHUNKS, 7)),
            dma((CHUNKS, 7)),
            dma((CHUNKS, 7)),
            dma((CHUNKS,)),
            dma((CHUNKS,)),
            dma((CHUNKS,)),
            dma((CHUNKS,)),
            dma((GROUPS,)),
            dma((GROUPS,)),
            dma((GROUPS,)),
            dma((GROUPS,)),
            dma((7,)),
            dma((7,)),
            pltpu.SemaphoreType.REGULAR,
            pltpu.SemaphoreType.REGULAR,
        ],
        compiler_params=pltpu.CompilerParams(
            collective_id=1, has_side_effects=True, vmem_limit_bytes=60 * 2**20
        ),
        name="galore_step",
    )(activations, cotangent, basis, weight, first_moment, second_moment)
    return pl.pallas_call(
        store,
        out_shape=tuple(jax.ShapeDtypeStruct(r.shape, r.dtype) for r in results),
        in_specs=[pl.BlockSpec(memory_space=pltpu.VMEM)] * 3,
        out_specs=(pl.BlockSpec(memory_space=pltpu.HBM),) * 3,
        scratch_shapes=[dma((3,))],
        compiler_params=pltpu.CompilerParams(vmem_limit_bytes=2 * 2**20),
        name="store_results",
    )(*results)


def solution(mesh):
    rows = P(("mp", "dp"), None)
    return jax.shard_map(
        body,
        mesh=mesh,
        in_specs=(P("dp", "mp"), P("dp", "mp"), P("mp", None), rows, rows, rows),
        out_specs=(rows, rows, rows),
        check_vma=False,
    )
```

```python
import functools

import jax
import jax.numpy as jnp
from jax import lax
from jax.experimental import pallas as pl
from jax.experimental.pallas import tpu as pltpu
from jax.sharding import PartitionSpec as P

STEP = 1000

beta_first = 0.9
beta_second = 0.999
adam_eps = 1e-08
step_rate = 0.1

MESH = pl.DeviceIdType.MESH
F32, BF16 = jnp.float32, jnp.bfloat16

TREES = (
    {4: 2, 3: 2, 2: 0, 1: 0, -3: -2, -2: 0, -1: 0},
    {4: 3, 3: 2, 2: 1, 1: 0, -3: -2, -2: -1, -1: 0},
)
SLOT = {o: i for i, o in enumerate(TREES[0])}
CHUNKS = 4
WIDTH = 1024 // CHUNKS
LIFT = 2.0**24
RING = (0, 1, 7, 2, 6, 3, 5, 4)
NEAR = 5


def children(tree, node):
    return [o for o in tree if tree[o] == node]


def height(tree, node):
    return 1 + max([height(tree, o) for o in children(tree, node)], default=-1)


def depth(tree, node):
    return 0 if node == 0 else 1 + depth(tree, tree[node])


def encode(value):
    return ((value * value) * (value * jnp.abs(value))).astype(BF16)


def decode(code):
    code = code.astype(F32)
    root = lax.rsqrt(jnp.maximum(jnp.abs(code), 1e-37))
    return code * (root * root) * lax.rsqrt(root)


def each(function, count=CHUNKS):
    lax.fori_loop(0, count, lambda c, carry: (function(c), carry)[1], 0)


def kernel(
    act_in, cot_in, basis_in, weight_in, first_in, second_in,
    weight_out, first_out, second_out,
    act, cot, basis, weight, first, second,
    partial, rs_send, rs_recv, proj, act_t, own, core_send, core_recv,
    x_send, x_recv, y_sum, y_send, y_recv, yf_send, yf_recv, xf_sum, xf_send, xf_recv, low, total, d_send, d_recv,
    load_sem, rs_ss, rs_rs, ag_ss, ag_rs, core_ss, core_rs, x_ss, x_rs, y_ss, y_rs, low_ss, low_rs, d_ss, d_rs,
    f_sem, near_sem, far_sem,
):
    dp, z = lax.axis_index("dp"), lax.axis_index("mp")
    y, x, core = dp // 8, (dp // 2) % 4, dp % 2
    sign = 1 - 2 * core

    def along_z(offset):
        return lax.rem(z + sign * offset + 16, 8)

    def at(y_to, x_to, core_to, z_to):
        return ((y_to * 4 + x_to) * 2 + core_to, z_to)

    def z_peer(offset):
        return at(y, x, core, along_z(offset))

    def x_peer(k):
        return at(y, lax.rem(x + k, 4), core, z)

    def y_peer(k):
        return at(lax.rem(y + k, 8), x, core, z)

    core_peer = at(y, x, 1 - core, z)

    def columns(c):
        return pl.ds(pl.multiple_of(c * WIDTH, WIDTH), WIDTH)

    barrier = pltpu.get_barrier_semaphore()
    peers = [z_peer(k) for k in (1, -1, 2, -2)] + [core_peer] + [x_peer(k) for k in (1, 3, 2)]
    peers += [y_peer(k) for k in (1, 7)]
    for peer in peers:
        pl.semaphore_signal(barrier, inc=1, device_id=peer, device_id_type=MESH)

    def load(i, source, target):
        return pltpu.make_async_copy(source, target, load_sem.at[i])

    cot_load = load(0, cot_in, cot)
    act_load = load(1, act_in, act)
    weight_load = load(2, weight_in, weight)
    first_load = load(3, first_in, first)
    second_load = load(4, second_in, second)

    def basis_load(c):
        return load(5 + c, basis_in.at[:, columns(c)], basis.at[c])

    cot_load.start()
    each(lambda c: basis_load(c).start())
    act_load.start()
    first_load.start()
    second_load.start()
    weight_load.start()

    def send(source, target, send_sem, recv_sem, peer):
        return pltpu.make_async_remote_copy(
            src_ref=source,
            dst_ref=target,
            send_sem=send_sem,
            recv_sem=recv_sem,
            device_id=peer,
            device_id_type=MESH,
        )

    def rs_copy(tree, c, o):
        i = SLOT[o]
        return send(rs_send.at[c, i], rs_recv.at[c, i], rs_ss.at[c, i], rs_rs.at[c, i], z_peer(tree[o] - o))

    def ag_copy(tree, c, o):
        i, block = SLOT[o], along_z(-tree[o])
        return send(proj.at[c, block], proj.at[c, block], ag_ss.at[c, i], ag_rs.at[c, i], z_peer(o - tree[o]))

    def core_copy(c):
        return send(core_send.at[c], core_recv.at[c], core_ss.at[c], core_rs.at[c], core_peer)

    def x_copy(c, k):
        return send(x_send.at[c, k - 1], x_recv.at[c, k - 1], x_ss.at[c], x_rs.at[c], x_peer(k))

    def x_all(c):
        return send(x_send.at[c], x_recv.at[c], x_ss.at[c], x_rs.at[c], x_peer(1))

    def y_copy(c, k):
        return send(y_send.at[c, k - 1], y_recv.at[c, k - 1], y_ss.at[c], y_rs.at[c], y_peer(k))

    def y_all(c):
        return send(y_send.at[c], y_recv.at[c], y_ss.at[c], y_rs.at[c], y_peer(1))

    def yf_copy(k):
        return send(yf_send.at[k - 1], yf_recv.at[k - 1], f_sem.at[0], f_sem.at[1], y_peer(k))

    def yf_all():
        return send(yf_send, yf_recv, f_sem.at[0], f_sem.at[1], y_peer(1))

    def xf_copy(k):
        return send(xf_send.at[k - 1], xf_recv.at[k - 1], f_sem.at[2], f_sem.at[3], x_peer(k))

    def xf_all():
        return send(xf_send, xf_recv, f_sem.at[2], f_sem.at[3], x_peer(1))

    def low_copy(c, i):
        part = int(i >= NEAR)
        return send(low.at[c, 0], low.at[c, i], low_ss.at[c], low_rs.at[c, part], z_peer(RING[i]))

    def low_part(c, part):
        some = low.at[c, pl.ds(*((1, NEAR - 1), (NEAR, 8 - NEAR))[part])]
        return send(some, some, low_ss.at[c], low_rs.at[c, part], z_peer(1))

    def d_copy(i):
        return send(d_send.at[i], d_recv.at[i - 1], d_ss.at[i - 1], d_rs.at[i - 1], z_peer(-RING[i]))

    def multiply(c):
        basis_load(c).wait()
        product = jnp.dot(cot[...], basis[c], preferred_element_type=F32)
        partial[c] = (product * LIFT).reshape(8, 64, WIDTH)

    def greet(semaphore, distance):
        for k in (distance, 8 - distance):
            pl.semaphore_signal(semaphore, inc=1, device_id=y_peer(k), device_id_type=MESH)

    def transpose(i):
        block = act[:, pl.ds(pl.multiple_of(i * 128, 128), 128)].T.reshape(4, 2, 16, 512)
        for j in range(4):
            for k in range(2):
                act_t[k, j, i] = block[j, k]

    def project(tree):
        late = [o for o in (1, -1) if tree[o] == 0 and height(tree, o) == 0]

        def arrived(c, o):
            rs_copy(tree, c, o).wait_recv()
            return decode(rs_recv[c, SLOT[o]])

        def rs_step(c, o):
            value = partial[c, along_z(-o)]
            for child in children(tree, o):
                value += arrived(c, child)
            rs_send[c, SLOT[o]] = encode(value)
            rs_copy(tree, c, o).start()

        def first_sends(c):
            @pl.when(c > 0)
            def _():
                multiply(c)

            for o in [o for o in tree if height(tree, o) == 0 and o not in late]:
                rs_step(c, o)

        each(first_sends)
        act_load.wait()
        lax.fori_loop(0, 8, lambda i, carry: (transpose(i), carry)[1], 0)
        greet(near_sem, 1)

        for level in range(1, height(tree, 0)):

            nodes = [o for o in tree if height(tree, o) == level] + [o for o in late if level == 1]

            def later_sends(c):
                for o in nodes:
                    rs_step(c, o)

            each(later_sends)

        def own_block(c):
            value = partial[c, z]
            for child in children(tree, 0):
                value += arrived(c, child)
            proj[c, z] = (value * (1.0 / LIFT)).astype(BF16)
            for o in children(tree, 0):
                ag_copy(tree, c, o).start()

        each(own_block)

        for level in range(1, max(depth(tree, o) for o in tree)):

            def forward(c):
                for o in tree:
                    if depth(tree, o) == level and children(tree, o):
                        ag_copy(tree, c, o).wait_recv()
                        for child in children(tree, o):
                            ag_copy(tree, c, child).start()

            each(forward)

    def wait_leaves(tree, c):
        for o in tree:
            if not children(tree, o):
                ag_copy(tree, c, o).wait_recv()

    cot_load.wait()
    multiply(0)
    pl.semaphore_wait(barrier, len(peers))

    for number, tree in enumerate(TREES):
        pl.when(core == number)(functools.partial(project, tree))

    def gradient(c):
        for number, tree in enumerate(TREES):
            pl.when(core == number)(functools.partial(wait_leaves, tree, c))
        here = proj[c].reshape(512, WIDTH)
        other = jnp.dot(act_t[1 - core].reshape(512, 512), here, preferred_element_type=F32)
        core_send[c] = other.reshape(4, 8, 16, WIDTH)
        core_copy(c).start()
        mine = jnp.dot(act_t[core].reshape(512, 512), here, preferred_element_type=F32)
        own[c] = mine.reshape(4, 8, 16, WIDTH)

    def y_first():
        core_copy(0).wait_recv()
        for k in (4, 3, 5, 2, 6, 1, 7):
            to = lax.rem(y + k, 8)
            yf_send[k - 1] = encode(own[0, :, to] + core_recv[0, :, to])
            yf_copy(k).start()

    def over_x(c):
        core_copy(c).wait_recv()
        for k in (2, 1, 3):
            to = lax.rem(x + k, 4)
            x_send[c, k - 1] = encode(own[c, to] + core_recv[c, to])
            x_copy(c, k).start()

    def over_y(c):
        value = own[c, x] + core_recv[c, x]
        x_all(c).wait_recv()
        for k in range(1, 4):
            value += decode(x_recv[c, k - 1])
        y_sum[c] = value
        for k in (4, 3, 5, 2, 6, 1, 7):
            y_send[c, k - 1] = encode(y_sum[c, lax.rem(y + k, 8)])
            y_copy(c, k).start()

    def x_second():
        value = own[0, :, y] + core_recv[0, :, y]
        yf_all().wait_recv()
        for k in range(1, 8):
            value += decode(yf_recv[k - 1])
        xf_sum[...] = value
        for k in (2, 1, 3):
            xf_send[k - 1] = encode(xf_sum[lax.rem(x + k, 4)])
            xf_copy(k).start()

    pl.semaphore_wait(near_sem, 2)
    greet(far_sem, 2)
    gradient(0)
    pl.semaphore_wait(far_sem, 2)
    y_first()

    def gradient_and_x(i):
        gradient(i + 1)
        over_x(i + 1)

    each(gradient_and_x, CHUNKS - 1)

    each(lambda i: over_y(i + 1), CHUNKS - 2)
    x_second()
    over_y(CHUNKS - 1)

    first_load.wait()
    second_load.wait()

    def grad_first():
        xf_all().wait_recv()
        grad = xf_sum[x]
        for k in range(1, 4):
            grad += decode(xf_recv[k - 1])
        return grad

    def grad_other(c):
        y_all(c).wait_recv()
        grad = y_sum[c, y]
        for k in range(1, 8):
            grad += decode(y_recv[c, k - 1])
        return grad

    def adam(c, grad):
        new_first = beta_first * first[:, columns(c)] + (1.0 - beta_first) * grad
        new_second = beta_second * second[:, columns(c)] + (1.0 - beta_second) * grad * grad
        first_out[:, columns(c)] = new_first
        second_out[:, columns(c)] = new_second
        first_hat = new_first / (1.0 - beta_first**STEP)
        second_hat = new_second / (1.0 - beta_second**STEP)
        low[c, 0] = (first_hat / (jnp.sqrt(second_hat) + adam_eps)).astype(BF16)
        for i in range(7, 0, -1):
            low_copy(c, i).start()

    each(lambda i: adam(i + 1, grad_other(i + 1)), CHUNKS - 2)
    adam(0, grad_first())
    adam(CHUNKS - 1, grad_other(CHUNKS - 1))

    def expand(start, size, part):
        rows = slice(16 * start, 16 * (start + size))
        total[rows] = jnp.zeros((16 * size, 1024), F32)

        def add(i):
            c = (i + 1) % (CHUNKS - 1) + (CHUNKS - 2) * (i // (CHUNKS - 1))
            low_part(c, part).wait_recv()
            total[rows] += lax.dot_general(
                low[c, start : start + size].reshape(16 * size, WIDTH),
                basis[c],
                (((1,), (1,)), ((), ())),
                preferred_element_type=F32,
            )

        each(add)
        d_send[start : start + size] = total[rows].astype(BF16).reshape(size, 16, 1024)
        for i in range(start + size - 1, max(start, 1) - 1, -1):
            d_copy(i).start()

    expand(0, NEAR, 0)
    expand(NEAR, 8 - NEAR, 1)

    def drain_z(tree, c):
        for o in tree:
            rs_copy(tree, c, o).wait_send()
            ag_copy(tree, c, o).wait_send()

    def drain(c):
        for number, tree in enumerate(TREES):
            pl.when(core == number)(functools.partial(drain_z, tree, c))
        core_copy(c).wait_send()
        low_part(c, 0).wait_send()
        low_part(c, 1).wait_send()

        @pl.when(c > 0)
        def _():
            x_all(c).wait_send()
            y_all(c).wait_send()

    each(drain)
    yf_all().wait_send()
    xf_all().wait_send()

    weight_load.wait()

    def update(block, delta):
        place = pl.ds(pl.multiple_of(block * 1024, 1024), 1024)
        value = weight[:, place].astype(F32) - step_rate * delta.astype(F32)
        weight_out[:, place] = value.astype(BF16)

    update(z, d_send[0])
    for i in range(1, 8):
        d_copy(i).wait_recv()
        update(along_z(RING[i]), d_recv[i - 1])
    for i in range(1, 8):
        d_copy(i).wait_send()


def store(weight, first, second, weight_out, first_out, second_out, sem):
    copies = [
        pltpu.make_async_copy(source, target, sem.at[i])
        for i, (source, target) in enumerate(((weight, weight_out), (first, first_out), (second, second_out)))
    ]
    for copy in copies:
        copy.start()
    for copy in copies:
        copy.wait()


def body(activations, cotangent, basis, weight, first_moment, second_moment):
    vmem, dma = pltpu.VMEM, pltpu.SemaphoreType.DMA
    results = pl.pallas_call(
        kernel,
        out_shape=(vmem((16, 8192), BF16), vmem((16, 1024), F32), vmem((16, 1024), F32)),
        in_specs=[pl.BlockSpec(memory_space=pltpu.HBM)] * 6,
        out_specs=(pl.BlockSpec(memory_space=pltpu.VMEM),) * 3,
        scratch_shapes=[
            vmem((512, 1024), BF16),
            vmem((512, 1024), BF16),
            vmem((CHUNKS, 1024, WIDTH), BF16),
            vmem((16, 8192), BF16),
            vmem((16, 1024), F32),
            vmem((16, 1024), F32),
            vmem((CHUNKS, 8, 64, WIDTH), F32),
            vmem((CHUNKS, 7, 64, WIDTH), BF16),
            vmem((CHUNKS, 7, 64, WIDTH), BF16),
            vmem((CHUNKS, 8, 64, WIDTH), BF16),
            vmem((2, 4, 8, 16, 512), BF16),
            vmem((CHUNKS, 4, 8, 16, WIDTH), F32),
            vmem((CHUNKS, 4, 8, 16, WIDTH), F32),
            vmem((CHUNKS, 4, 8, 16, WIDTH), F32),
            vmem((CHUNKS, 3, 8, 16, WIDTH), BF16),
            vmem((CHUNKS, 3, 8, 16, WIDTH), BF16),
            vmem((CHUNKS, 8, 16, WIDTH), F32),
            vmem((CHUNKS, 7, 16, WIDTH), BF16),
            vmem((CHUNKS, 7, 16, WIDTH), BF16),
            vmem((7, 4, 16, WIDTH), BF16),
            vmem((7, 4, 16, WIDTH), BF16),
            vmem((4, 16, WIDTH), F32),
            vmem((3, 16, WIDTH), BF16),
            vmem((3, 16, WIDTH), BF16),
            vmem((CHUNKS, 8, 16, WIDTH), BF16),
            vmem((128, 1024), F32),
            vmem((8, 16, 1024), BF16),
            vmem((7, 16, 1024), BF16),
            dma((5 + CHUNKS,)),
            dma((CHUNKS, 7)),
            dma((CHUNKS, 7)),
            dma((CHUNKS, 7)),
            dma((CHUNKS, 7)),
            dma((CHUNKS,)),
            dma((CHUNKS,)),
            dma((CHUNKS,)),
            dma((CHUNKS,)),
            dma((CHUNKS,)),
            dma((CHUNKS,)),
            dma((CHUNKS,)),
            dma((CHUNKS, 2)),
            dma((7,)),
            dma((7,)),
            dma((4,)),
            pltpu.SemaphoreType.REGULAR,
            pltpu.SemaphoreType.REGULAR,
        ],
        compiler_params=pltpu.CompilerParams(
            collective_id=1, has_side_effects=True, vmem_limit_bytes=60 * 2**20
        ),
        name="galore_step",
    )(activations, cotangent, basis, weight, first_moment, second_moment)
    return pl.pallas_call(
        store,
        out_shape=tuple(jax.ShapeDtypeStruct(r.shape, r.dtype) for r in results),
        in_specs=[pl.BlockSpec(memory_space=pltpu.VMEM)] * 3,
        out_specs=(pl.BlockSpec(memory_space=pltpu.HBM),) * 3,
        scratch_shapes=[dma((3,))],
        compiler_params=pltpu.CompilerParams(vmem_limit_bytes=2 * 2**20),
        name="store_results",
    )(*results)


def solution(mesh):
    rows = P(("mp", "dp"), None)
    return jax.shard_map(
        body,
        mesh=mesh,
        in_specs=(P("dp", "mp"), P("dp", "mp"), P("mp", None), rows, rows, rows),
        out_specs=(rows, rows, rows),
        check_vma=False,
    )
```

```python
import functools

import jax
import jax.numpy as jnp
from jax import lax
from jax.experimental import pallas as pl
from jax.experimental.pallas import tpu as pltpu
from jax.sharding import PartitionSpec as P

STEP = 1000

beta_first = 0.9
beta_second = 0.999
adam_eps = 1e-08
step_rate = 0.1

MESH = pl.DeviceIdType.MESH
F32, BF16 = jnp.float32, jnp.bfloat16

TREES = (
    {4: 2, 3: 2, 2: 0, 1: 0, -3: -2, -2: 0, -1: 0},
    {4: 3, 3: 2, 2: 1, 1: 0, -3: -2, -2: -1, -1: 0},
)
SLOT = {o: i for i, o in enumerate(TREES[0])}
CHUNKS = 4
WIDTH = 1024 // CHUNKS
LIFT = 2.0**24
RING = (0, 1, 7, 2, 6, 3, 5, 4)
NEAR = 5


def children(tree, node):
    return [o for o in tree if tree[o] == node]


def height(tree, node):
    return 1 + max([height(tree, o) for o in children(tree, node)], default=-1)


def depth(tree, node):
    return 0 if node == 0 else 1 + depth(tree, tree[node])


def encode(value):
    return ((value * value) * (value * jnp.abs(value))).astype(BF16)


def decode(code):
    code = code.astype(F32)
    root = lax.rsqrt(jnp.maximum(jnp.abs(code), 1e-37))
    return code * (root * root) * lax.rsqrt(root)


def each(function, count=CHUNKS):
    lax.fori_loop(0, count, lambda c, carry: (function(c), carry)[1], 0)


def kernel(
    act_in, cot_in, basis_in, weight_in, first_in, second_in,
    weight_out, first_out, second_out,
    act, cot, basis, weight, first, second,
    partial, rs_send, rs_recv, proj, act_t, own, core_send, core_recv,
    x_send, x_recv, y_sum, y_send, y_recv, yf_send, yf_recv, xf_sum, xf_send, xf_recv, low, total, d_send, d_recv,
    load_sem, rs_ss, rs_rs, ag_ss, ag_rs, core_ss, core_rs, x_ss, x_rs, y_ss, y_rs, low_ss, low_rs, d_ss, d_rs,
    f_sem, near_sem, far_sem,
):
    dp, z = lax.axis_index("dp"), lax.axis_index("mp")
    y, x, core = dp // 8, (dp // 2) % 4, dp % 2
    sign = 1 - 2 * core

    def along_z(offset):
        return lax.rem(z + sign * offset + 16, 8)

    def at(y_to, x_to, core_to, z_to):
        return ((y_to * 4 + x_to) * 2 + core_to, z_to)

    def z_peer(offset):
        return at(y, x, core, along_z(offset))

    def x_peer(k):
        return at(y, lax.rem(x + k, 4), core, z)

    def y_peer(k):
        return at(lax.rem(y + k, 8), x, core, z)

    core_peer = at(y, x, 1 - core, z)

    def columns(c):
        return pl.ds(pl.multiple_of(c * WIDTH, WIDTH), WIDTH)

    barrier = pltpu.get_barrier_semaphore()
    peers = [z_peer(k) for k in (2, -2, 1, -1)] + [core_peer] + [x_peer(k) for k in (1, 3, 2)]
    peers += [y_peer(k) for k in (1, 7)]
    for peer in peers:
        pl.semaphore_signal(barrier, inc=1, device_id=peer, device_id_type=MESH)

    def load(i, source, target):
        return pltpu.make_async_copy(source, target, load_sem.at[i])

    cot_load = load(0, cot_in, cot)
    act_load = load(1, act_in, act)
    weight_load = load(2, weight_in, weight)
    first_load = load(3, first_in, first)
    second_load = load(4, second_in, second)

    def basis_load(c):
        return load(5 + c, basis_in.at[:, columns(c)], basis.at[c])

    cot_load.start()
    each(lambda c: basis_load(c).start())
    act_load.start()
    first_load.start()
    second_load.start()
    weight_load.start()

    def send(source, target, send_sem, recv_sem, peer):
        return pltpu.make_async_remote_copy(
            src_ref=source,
            dst_ref=target,
            send_sem=send_sem,
            recv_sem=recv_sem,
            device_id=peer,
            device_id_type=MESH,
        )

    def rs_copy(tree, c, o):
        i = SLOT[o]
        return send(rs_send.at[c, i], rs_recv.at[c, i], rs_ss.at[c, i], rs_rs.at[c, i], z_peer(tree[o] - o))

    def ag_copy(tree, c, o):
        i, block = SLOT[o], along_z(-tree[o])
        return send(proj.at[c, block], proj.at[c, block], ag_ss.at[c, i], ag_rs.at[c, i], z_peer(o - tree[o]))

    def core_copy(c):
        return send(core_send.at[c], core_recv.at[c], core_ss.at[c], core_rs.at[c], core_peer)

    def x_copy(c, k):
        return send(x_send.at[c, k - 1], x_recv.at[c, k - 1], x_ss.at[c], x_rs.at[c], x_peer(k))

    def x_all(c):
        return send(x_send.at[c], x_recv.at[c], x_ss.at[c], x_rs.at[c], x_peer(1))

    def y_copy(c, k):
        return send(y_send.at[c, k - 1], y_recv.at[c, k - 1], y_ss.at[c], y_rs.at[c], y_peer(k))

    def y_all(c):
        return send(y_send.at[c], y_recv.at[c], y_ss.at[c], y_rs.at[c], y_peer(1))

    def yf_copy(k):
        return send(yf_send.at[k - 1], yf_recv.at[k - 1], f_sem.at[0], f_sem.at[1], y_peer(k))

    def yf_all():
        return send(yf_send, yf_recv, f_sem.at[0], f_sem.at[1], y_peer(1))

    def xf_copy(k):
        return send(xf_send.at[k - 1], xf_recv.at[k - 1], f_sem.at[2], f_sem.at[3], x_peer(k))

    def xf_all():
        return send(xf_send, xf_recv, f_sem.at[2], f_sem.at[3], x_peer(1))

    def low_copy(c, i):
        part = int(i >= NEAR)
        return send(low.at[c, 0], low.at[c, i], low_ss.at[c], low_rs.at[c, part], z_peer(RING[i]))

    def low_part(c, part):
        some = low.at[c, pl.ds(*((1, NEAR - 1), (NEAR, 8 - NEAR))[part])]
        return send(some, some, low_ss.at[c], low_rs.at[c, part], z_peer(1))

    def d_copy(i):
        return send(d_send.at[i], d_recv.at[i - 1], d_ss.at[i - 1], d_rs.at[i - 1], z_peer(-RING[i]))

    def multiply(c):
        basis_load(c).wait()
        product = jnp.dot(cot[...], basis[c], preferred_element_type=F32)
        partial[c] = (product * LIFT).reshape(8, 64, WIDTH)

    def greet(semaphore, distance):
        for k in (distance, 8 - distance):
            pl.semaphore_signal(semaphore, inc=1, device_id=y_peer(k), device_id_type=MESH)

    def transpose(i):
        block = act[:, pl.ds(pl.multiple_of(i * 128, 128), 128)].T.reshape(4, 2, 16, 512)
        for j in range(4):
            for k in range(2):
                act_t[k, j, i] = block[j, k]

    def project(tree):
        late = [o for o in (1, -1) if tree[o] == 0 and height(tree, o) == 0]

        def arrived(c, o):
            rs_copy(tree, c, o).wait_recv()
            return decode(rs_recv[c, SLOT[o]])

        def rs_step(c, o):
            value = partial[c, along_z(-o)]
            for child in children(tree, o):
                value += arrived(c, child)
            rs_send[c, SLOT[o]] = encode(value)
            rs_copy(tree, c, o).start()

        def first_sends(c):
            @pl.when(c > 0)
            def _():
                multiply(c)

            for o in [o for o in tree if height(tree, o) == 0 and o not in late]:
                rs_step(c, o)

        each(first_sends)
        act_load.wait()
        lax.fori_loop(0, 8, lambda i, carry: (transpose(i), carry)[1], 0)
        greet(near_sem, 1)

        for level in range(1, height(tree, 0)):

            nodes = [o for o in tree if height(tree, o) == level] + [o for o in late if level == 1]

            def later_sends(c):
                for o in nodes:
                    rs_step(c, o)

            each(later_sends)

        def own_block(c):
            value = partial[c, z]
            for child in children(tree, 0):
                value += arrived(c, child)
            proj[c, z] = (value * (1.0 / LIFT)).astype(BF16)
            for o in children(tree, 0):
                if o not in late:
                    ag_copy(tree, c, o).start()

        each(own_block)

        for level in range(1, max(depth(tree, o) for o in tree)):

            def forward(c):
                for o in tree:
                    if depth(tree, o) == level and children(tree, o):
                        ag_copy(tree, c, o).wait_recv()
                        for child in children(tree, o):
                            ag_copy(tree, c, child).start()
                if level == 1:
                    for o in late:
                        ag_copy(tree, c, o).start()

            each(forward)

    def wait_leaves(tree, c):
        for o in tree:
            if not children(tree, o):
                ag_copy(tree, c, o).wait_recv()

    cot_load.wait()
    multiply(0)
    pl.semaphore_wait(barrier, len(peers))

    for number, tree in enumerate(TREES):
        pl.when(core == number)(functools.partial(project, tree))

    def gradient(c):
        for number, tree in enumerate(TREES):
            pl.when(core == number)(functools.partial(wait_leaves, tree, c))
        here = proj[c].reshape(512, WIDTH)
        other = jnp.dot(act_t[1 - core].reshape(512, 512), here, preferred_element_type=F32)
        core_send[c] = other.reshape(4, 8, 16, WIDTH)
        core_copy(c).start()
        mine = jnp.dot(act_t[core].reshape(512, 512), here, preferred_element_type=F32)
        own[c] = mine.reshape(4, 8, 16, WIDTH)

    def y_first():
        core_copy(0).wait_recv()
        for k in (4, 3, 5, 2, 6, 1, 7):
            to = lax.rem(y + k, 8)
            yf_send[k - 1] = encode(own[0, :, to] + core_recv[0, :, to])
            yf_copy(k).start()

    def over_x(c):
        core_copy(c).wait_recv()
        for k in (2, 1, 3):
            to = lax.rem(x + k, 4)
            x_send[c, k - 1] = encode(own[c, to] + core_recv[c, to])
            x_copy(c, k).start()

    def over_y(c):
        value = own[c, x] + core_recv[c, x]
        x_all(c).wait_recv()
        for k in range(1, 4):
            value += decode(x_recv[c, k - 1])
        y_sum[c] = value
        for k in (4, 3, 5, 2, 6, 1, 7):
            y_send[c, k - 1] = encode(y_sum[c, lax.rem(y + k, 8)])
            y_copy(c, k).start()

    def x_second():
        value = own[0, :, y] + core_recv[0, :, y]
        yf_all().wait_recv()
        for k in range(1, 8):
            value += decode(yf_recv[k - 1])
        xf_sum[...] = value
        for k in (2, 1, 3):
            xf_send[k - 1] = encode(xf_sum[lax.rem(x + k, 4)])
            xf_copy(k).start()

    pl.semaphore_wait(near_sem, 2)
    greet(far_sem, 2)
    gradient(0)
    pl.semaphore_wait(far_sem, 2)
    y_first()

    def gradient_and_x(i):
        gradient(i + 1)
        over_x(i + 1)

    each(gradient_and_x, CHUNKS - 1)

    each(lambda i: over_y(i + 1), CHUNKS - 2)
    x_second()
    over_y(CHUNKS - 1)

    first_load.wait()
    second_load.wait()

    def grad_first():
        xf_all().wait_recv()
        grad = xf_sum[x]
        for k in range(1, 4):
            grad += decode(xf_recv[k - 1])
        return grad

    def grad_other(c):
        y_all(c).wait_recv()
        grad = y_sum[c, y]
        for k in range(1, 8):
            grad += decode(y_recv[c, k - 1])
        return grad

    def adam(c, grad):
        new_first = beta_first * first[:, columns(c)] + (1.0 - beta_first) * grad
        new_second = beta_second * second[:, columns(c)] + (1.0 - beta_second) * grad * grad
        first_out[:, columns(c)] = new_first
        second_out[:, columns(c)] = new_second
        first_hat = new_first / (1.0 - beta_first**STEP)
        second_hat = new_second / (1.0 - beta_second**STEP)
        low[c, 0] = (first_hat / (jnp.sqrt(second_hat) + adam_eps)).astype(BF16)
        for i in range(7, 0, -1):
            low_copy(c, i).start()

    each(lambda i: adam(i + 1, grad_other(i + 1)), CHUNKS - 2)
    adam(0, grad_first())
    adam(CHUNKS - 1, grad_other(CHUNKS - 1))

    def expand(start, size, part):
        rows = slice(16 * start, 16 * (start + size))
        total[rows] = jnp.zeros((16 * size, 1024), F32)

        def add(i):
            c = (i + 1) % (CHUNKS - 1) + (CHUNKS - 2) * (i // (CHUNKS - 1))
            low_part(c, part).wait_recv()
            total[rows] += lax.dot_general(
                low[c, start : start + size].reshape(16 * size, WIDTH),
                basis[c],
                (((1,), (1,)), ((), ())),
                preferred_element_type=F32,
            )

        each(add)
        d_send[start : start + size] = total[rows].astype(BF16).reshape(size, 16, 1024)
        for i in range(start + size - 1, max(start, 1) - 1, -1):
            d_copy(i).start()

    expand(0, NEAR, 0)
    expand(NEAR, 8 - NEAR, 1)

    def drain_z(tree, c):
        for o in tree:
            rs_copy(tree, c, o).wait_send()
            ag_copy(tree, c, o).wait_send()

    def drain(c):
        for number, tree in enumerate(TREES):
            pl.when(core == number)(functools.partial(drain_z, tree, c))
        core_copy(c).wait_send()
        low_part(c, 0).wait_send()
        low_part(c, 1).wait_send()

        @pl.when(c > 0)
        def _():
            x_all(c).wait_send()
            y_all(c).wait_send()

    each(drain)
    yf_all().wait_send()
    xf_all().wait_send()

    weight_load.wait()

    def update(block, delta):
        place = pl.ds(pl.multiple_of(block * 1024, 1024), 1024)
        value = weight[:, place].astype(F32) - step_rate * delta.astype(F32)
        weight_out[:, place] = value.astype(BF16)

    update(z, d_send[0])
    for i in range(1, 8):
        d_copy(i).wait_recv()
        update(along_z(RING[i]), d_recv[i - 1])
    for i in range(1, 8):
        d_copy(i).wait_send()


def store(weight, first, second, weight_out, first_out, second_out, sem):
    copies = [
        pltpu.make_async_copy(source, target, sem.at[i])
        for i, (source, target) in enumerate(((weight, weight_out), (first, first_out), (second, second_out)))
    ]
    for copy in copies:
        copy.start()
    for copy in copies:
        copy.wait()


def body(activations, cotangent, basis, weight, first_moment, second_moment):
    vmem, dma = pltpu.VMEM, pltpu.SemaphoreType.DMA
    results = pl.pallas_call(
        kernel,
        out_shape=(vmem((16, 8192), BF16), vmem((16, 1024), F32), vmem((16, 1024), F32)),
        in_specs=[pl.BlockSpec(memory_space=pltpu.HBM)] * 6,
        out_specs=(pl.BlockSpec(memory_space=pltpu.VMEM),) * 3,
        scratch_shapes=[
            vmem((512, 1024), BF16),
            vmem((512, 1024), BF16),
            vmem((CHUNKS, 1024, WIDTH), BF16),
            vmem((16, 8192), BF16),
            vmem((16, 1024), F32),
            vmem((16, 1024), F32),
            vmem((CHUNKS, 8, 64, WIDTH), F32),
            vmem((CHUNKS, 7, 64, WIDTH), BF16),
            vmem((CHUNKS, 7, 64, WIDTH), BF16),
            vmem((CHUNKS, 8, 64, WIDTH), BF16),
            vmem((2, 4, 8, 16, 512), BF16),
            vmem((CHUNKS, 4, 8, 16, WIDTH), F32),
            vmem((CHUNKS, 4, 8, 16, WIDTH), F32),
            vmem((CHUNKS, 4, 8, 16, WIDTH), F32),
            vmem((CHUNKS, 3, 8, 16, WIDTH), BF16),
            vmem((CHUNKS, 3, 8, 16, WIDTH), BF16),
            vmem((CHUNKS, 8, 16, WIDTH), F32),
            vmem((CHUNKS, 7, 16, WIDTH), BF16),
            vmem((CHUNKS, 7, 16, WIDTH), BF16),
            vmem((7, 4, 16, WIDTH), BF16),
            vmem((7, 4, 16, WIDTH), BF16),
            vmem((4, 16, WIDTH), F32),
            vmem((3, 16, WIDTH), BF16),
            vmem((3, 16, WIDTH), BF16),
            vmem((CHUNKS, 8, 16, WIDTH), BF16),
            vmem((128, 1024), F32),
            vmem((8, 16, 1024), BF16),
            vmem((7, 16, 1024), BF16),
            dma((5 + CHUNKS,)),
            dma((CHUNKS, 7)),
            dma((CHUNKS, 7)),
            dma((CHUNKS, 7)),
            dma((CHUNKS, 7)),
            dma((CHUNKS,)),
            dma((CHUNKS,)),
            dma((CHUNKS,)),
            dma((CHUNKS,)),
            dma((CHUNKS,)),
            dma((CHUNKS,)),
            dma((CHUNKS,)),
            dma((CHUNKS, 2)),
            dma((7,)),
            dma((7,)),
            dma((4,)),
            pltpu.SemaphoreType.REGULAR,
            pltpu.SemaphoreType.REGULAR,
        ],
        compiler_params=pltpu.CompilerParams(
            collective_id=1, has_side_effects=True, vmem_limit_bytes=60 * 2**20
        ),
        name="galore_step",
    )(activations, cotangent, basis, weight, first_moment, second_moment)
    return pl.pallas_call(
        store,
        out_shape=tuple(jax.ShapeDtypeStruct(r.shape, r.dtype) for r in results),
        in_specs=[pl.BlockSpec(memory_space=pltpu.VMEM)] * 3,
        out_specs=(pl.BlockSpec(memory_space=pltpu.HBM),) * 3,
        scratch_shapes=[dma((3,))],
        compiler_params=pltpu.CompilerParams(vmem_limit_bytes=2 * 2**20),
        name="store_results",
    )(*results)


def solution(mesh):
    rows = P(("mp", "dp"), None)
    return jax.shard_map(
        body,
        mesh=mesh,
        in_specs=(P("dp", "mp"), P("dp", "mp"), P("mp", None), rows, rows, rows),
        out_specs=(rows, rows, rows),
        check_vma=False,
    )
```

```python
import functools

import jax
import jax.numpy as jnp
from jax import lax
from jax.experimental import pallas as pl
from jax.experimental.pallas import tpu as pltpu
from jax.sharding import PartitionSpec as P

STEP = 1000

beta_first = 0.9
beta_second = 0.999
adam_eps = 1e-08
step_rate = 0.1

MESH = pl.DeviceIdType.MESH
F32, BF16 = jnp.float32, jnp.bfloat16

TREES = (
    {4: 2, 3: 2, 2: 0, 1: 0, -3: -2, -2: 0, -1: 0},
    {4: 3, 3: 2, 2: 1, 1: 0, -3: -2, -2: -1, -1: 0},
)
SLOT = {o: i for i, o in enumerate(TREES[0])}
CHUNKS = 4
WIDTH = 1024 // CHUNKS
LIFT = 2.0**24
RING = (0, 1, 7, 2, 6, 3, 5, 4)
NEAR = 5


def children(tree, node):
    return [o for o in tree if tree[o] == node]


def height(tree, node):
    return 1 + max([height(tree, o) for o in children(tree, node)], default=-1)


def depth(tree, node):
    return 0 if node == 0 else 1 + depth(tree, tree[node])


def encode(value):
    return ((value * value) * (value * jnp.abs(value))).astype(BF16)


def decode(code):
    code = code.astype(F32)
    root = lax.rsqrt(jnp.maximum(jnp.abs(code), 1e-37))
    return code * (root * root) * lax.rsqrt(root)


def each(function, count=CHUNKS):
    lax.fori_loop(0, count, lambda c, carry: (function(c), carry)[1], 0)


def kernel(
    act_in, cot_in, basis_in, weight_in, first_in, second_in,
    weight_out, first_out, second_out,
    act, cot, basis, weight, first, second,
    partial, rs_send, rs_recv, proj, act_t, own, core_send, core_recv,
    x_send, x_recv, y_sum, y_send, y_recv, yf_send, yf_recv, xf_sum, xf_send, xf_recv, low, total, d_send, d_recv,
    load_sem, rs_ss, rs_rs, ag_ss, ag_rs, core_ss, core_rs, x_ss, x_rs, y_ss, y_rs, low_ss, low_rs, d_ss, d_rs,
    f_sem, near_sem, far_sem,
):
    dp, z = lax.axis_index("dp"), lax.axis_index("mp")
    y, x, core = dp // 8, (dp // 2) % 4, dp % 2
    sign = 1 - 2 * core

    def along_z(offset):
        return lax.rem(z + sign * offset + 16, 8)

    def at(y_to, x_to, core_to, z_to):
        return ((y_to * 4 + x_to) * 2 + core_to, z_to)

    def z_peer(offset):
        return at(y, x, core, along_z(offset))

    def x_peer(k):
        return at(y, lax.rem(x + k, 4), core, z)

    def y_peer(k):
        return at(lax.rem(y + k, 8), x, core, z)

    core_peer = at(y, x, 1 - core, z)

    def columns(c):
        return pl.ds(pl.multiple_of(c * WIDTH, WIDTH), WIDTH)

    barrier = pltpu.get_barrier_semaphore()
    peers = [z_peer(k) for k in (2, -2, 1, -1)] + [core_peer] + [x_peer(k) for k in (1, 3, 2)]
    peers += [y_peer(k) for k in (1, 7)]
    for peer in peers:
        pl.semaphore_signal(barrier, inc=1, device_id=peer, device_id_type=MESH)

    def load(i, source, target):
        return pltpu.make_async_copy(source, target, load_sem.at[i])

    cot_load = load(0, cot_in, cot)
    act_load = load(1, act_in, act)
    weight_load = load(2, weight_in, weight)
    first_load = load(3, first_in, first)
    second_load = load(4, second_in, second)

    def basis_load(c):
        return load(5 + c, basis_in.at[:, columns(c)], basis.at[c])

    cot_load.start()
    each(lambda c: basis_load(c).start())
    act_load.start()
    first_load.start()
    second_load.start()
    weight_load.start()

    def send(source, target, send_sem, recv_sem, peer):
        return pltpu.make_async_remote_copy(
            src_ref=source,
            dst_ref=target,
            send_sem=send_sem,
            recv_sem=recv_sem,
            device_id=peer,
            device_id_type=MESH,
        )

    def rs_copy(tree, c, o):
        i = SLOT[o]
        return send(rs_send.at[c, i], rs_recv.at[c, i], rs_ss.at[c, i], rs_rs.at[c, i], z_peer(tree[o] - o))

    def ag_copy(tree, c, o):
        i, block = SLOT[o], along_z(-tree[o])
        return send(proj.at[c, block], proj.at[c, block], ag_ss.at[c, i], ag_rs.at[c, i], z_peer(o - tree[o]))

    def core_copy(c):
        return send(core_send.at[c], core_recv.at[c], core_ss.at[c], core_rs.at[c], core_peer)

    def x_copy(c, k):
        return send(x_send.at[c, k - 1], x_recv.at[c, k - 1], x_ss.at[c], x_rs.at[c], x_peer(k))

    def x_all(c):
        return send(x_send.at[c], x_recv.at[c], x_ss.at[c], x_rs.at[c], x_peer(1))

    def y_copy(c, k):
        return send(y_send.at[c, k - 1], y_recv.at[c, k - 1], y_ss.at[c], y_rs.at[c], y_peer(k))

    def y_all(c):
        return send(y_send.at[c], y_recv.at[c], y_ss.at[c], y_rs.at[c], y_peer(1))

    def yf_copy(k):
        return send(yf_send.at[k - 1], yf_recv.at[k - 1], f_sem.at[0], f_sem.at[1], y_peer(k))

    def yf_all():
        return send(yf_send, yf_recv, f_sem.at[0], f_sem.at[1], y_peer(1))

    def xf_copy(k):
        return send(xf_send.at[k - 1], xf_recv.at[k - 1], f_sem.at[2], f_sem.at[3], x_peer(k))

    def xf_all():
        return send(xf_send, xf_recv, f_sem.at[2], f_sem.at[3], x_peer(1))

    def low_copy(c, i):
        part = int(i >= NEAR)
        return send(low.at[c, 0], low.at[c, i], low_ss.at[c], low_rs.at[c, part], z_peer(RING[i]))

    def low_part(c, part):
        some = low.at[c, pl.ds(*((1, NEAR - 1), (NEAR, 8 - NEAR))[part])]
        return send(some, some, low_ss.at[c], low_rs.at[c, part], z_peer(1))

    def d_copy(i):
        return send(d_send.at[i], d_recv.at[i - 1], d_ss.at[i - 1], d_rs.at[i - 1], z_peer(-RING[i]))

    def multiply(c):
        basis_load(c).wait()
        product = jnp.dot(cot[...], basis[c], preferred_element_type=F32)
        partial[c] = (product * LIFT).reshape(8, 64, WIDTH)

    def greet(semaphore, distance):
        for k in (distance, 8 - distance):
            pl.semaphore_signal(semaphore, inc=1, device_id=y_peer(k), device_id_type=MESH)

    def transpose(i):
        block = act[:, pl.ds(pl.multiple_of(i * 128, 128), 128)].T.reshape(4, 2, 16, 512)
        for j in range(4):
            for k in range(2):
                act_t[k, j, i] = block[j, k]

    def project(tree):
        late = [o for o in (1, -1) if tree[o] == 0 and height(tree, o) == 0]

        def arrived(c, o):
            rs_copy(tree, c, o).wait_recv()
            return decode(rs_recv[c, SLOT[o]])

        def rs_step(c, o):
            value = partial[c, along_z(-o)]
            for child in children(tree, o):
                value += arrived(c, child)
            rs_send[c, SLOT[o]] = encode(value)
            rs_copy(tree, c, o).start()

        def first_sends(c):
            @pl.when(c > 0)
            def _():
                multiply(c)

            for o in [o for o in tree if height(tree, o) == 0 and o not in late]:
                rs_step(c, o)

        each(first_sends)
        act_load.wait()
        lax.fori_loop(0, 8, lambda i, carry: (transpose(i), carry)[1], 0)
        greet(near_sem, 1)

        for level in range(1, height(tree, 0)):

            nodes = [o for o in tree if height(tree, o) == level] + [o for o in late if level == 1]

            def later_sends(c):
                for o in nodes:
                    rs_step(c, o)

            each(later_sends)

        def own_block(c):
            value = partial[c, z]
            for child in children(tree, 0):
                value += arrived(c, child)
            proj[c, z] = (value * (1.0 / LIFT)).astype(BF16)
            for o in children(tree, 0):
                if o not in late:
                    ag_copy(tree, c, o).start()

        each(own_block)

        for level in range(1, max(depth(tree, o) for o in tree)):

            def forward(c):
                for o in tree:
                    if depth(tree, o) == level and children(tree, o):
                        ag_copy(tree, c, o).wait_recv()
                        for child in children(tree, o):
                            ag_copy(tree, c, child).start()
                if level == 1:
                    for o in late:
                        ag_copy(tree, c, o).start()

            each(forward)

    def wait_leaves(tree, c):
        for o in tree:
            if not children(tree, o):
                ag_copy(tree, c, o).wait_recv()

    cot_load.wait()
    multiply(0)
    pl.semaphore_wait(barrier, len(peers))

    for number, tree in enumerate(TREES):
        pl.when(core == number)(functools.partial(project, tree))

    def gradient(c):
        for number, tree in enumerate(TREES):
            pl.when(core == number)(functools.partial(wait_leaves, tree, c))
        here = proj[c].reshape(512, WIDTH)
        other = jnp.dot(act_t[1 - core].reshape(512, 512), here, preferred_element_type=F32)
        core_send[c] = encode(other).reshape(4, 8, 16, WIDTH)
        core_copy(c).start()
        mine = jnp.dot(act_t[core].reshape(512, 512), here, preferred_element_type=F32)
        own[c] = mine.reshape(4, 8, 16, WIDTH)

    def y_first():
        core_copy(0).wait_recv()
        for k in (4, 3, 5, 2, 6, 1, 7):
            to = lax.rem(y + k, 8)
            yf_send[k - 1] = encode(own[0, :, to] + decode(core_recv[0, :, to]))
            yf_copy(k).start()

    def over_x(c):
        core_copy(c).wait_recv()
        for k in (2, 1, 3):
            to = lax.rem(x + k, 4)
            x_send[c, k - 1] = encode(own[c, to] + decode(core_recv[c, to]))
            x_copy(c, k).start()

    def over_y(c):
        value = own[c, x] + decode(core_recv[c, x])
        x_all(c).wait_recv()
        for k in range(1, 4):
            value += decode(x_recv[c, k - 1])
        y_sum[c] = value
        for k in (4, 3, 5, 2, 6, 1, 7):
            y_send[c, k - 1] = encode(y_sum[c, lax.rem(y + k, 8)])
            y_copy(c, k).start()

    def x_second():
        value = own[0, :, y] + decode(core_recv[0, :, y])
        yf_all().wait_recv()
        for k in range(1, 8):
            value += decode(yf_recv[k - 1])
        xf_sum[...] = value
        for k in (2, 1, 3):
            xf_send[k - 1] = encode(xf_sum[lax.rem(x + k, 4)])
            xf_copy(k).start()

    pl.semaphore_wait(near_sem, 2)
    greet(far_sem, 2)
    gradient(0)
    pl.semaphore_wait(far_sem, 2)
    y_first()

    def gradient_and_x(i):
        gradient(i + 1)
        over_x(i + 1)

    each(gradient_and_x, CHUNKS - 1)

    each(lambda i: over_y(i + 1), CHUNKS - 2)
    x_second()
    over_y(CHUNKS - 1)

    first_load.wait()
    second_load.wait()

    def grad_first():
        xf_all().wait_recv()
        grad = xf_sum[x]
        for k in range(1, 4):
            grad += decode(xf_recv[k - 1])
        return grad

    def grad_other(c):
        y_all(c).wait_recv()
        grad = y_sum[c, y]
        for k in range(1, 8):
            grad += decode(y_recv[c, k - 1])
        return grad

    def adam(c, grad):
        new_first = beta_first * first[:, columns(c)] + (1.0 - beta_first) * grad
        new_second = beta_second * second[:, columns(c)] + (1.0 - beta_second) * grad * grad
        first_out[:, columns(c)] = new_first
        second_out[:, columns(c)] = new_second
        first_hat = new_first / (1.0 - beta_first**STEP)
        second_hat = new_second / (1.0 - beta_second**STEP)
        low[c, 0] = (first_hat / (jnp.sqrt(second_hat) + adam_eps)).astype(BF16)
        for i in range(7, 0, -1):
            low_copy(c, i).start()

    each(lambda i: adam(i + 1, grad_other(i + 1)), CHUNKS - 2)
    adam(0, grad_first())
    adam(CHUNKS - 1, grad_other(CHUNKS - 1))

    def expand(start, size, part):
        rows = slice(16 * start, 16 * (start + size))
        total[rows] = jnp.zeros((16 * size, 1024), F32)

        def add(i):
            c = (i + 1) % (CHUNKS - 1) + (CHUNKS - 2) * (i // (CHUNKS - 1))
            low_part(c, part).wait_recv()
            total[rows] += lax.dot_general(
                low[c, start : start + size].reshape(16 * size, WIDTH),
                basis[c],
                (((1,), (1,)), ((), ())),
                preferred_element_type=F32,
            )

        each(add)
        d_send[start : start + size] = total[rows].astype(BF16).reshape(size, 16, 1024)
        for i in range(start + size - 1, max(start, 1) - 1, -1):
            d_copy(i).start()

    expand(0, NEAR, 0)
    expand(NEAR, 8 - NEAR, 1)

    def drain_z(tree, c):
        for o in tree:
            rs_copy(tree, c, o).wait_send()
            ag_copy(tree, c, o).wait_send()

    def drain(c):
        for number, tree in enumerate(TREES):
            pl.when(core == number)(functools.partial(drain_z, tree, c))
        core_copy(c).wait_send()
        low_part(c, 0).wait_send()
        low_part(c, 1).wait_send()

        @pl.when(c > 0)
        def _():
            x_all(c).wait_send()
            y_all(c).wait_send()

    each(drain)
    yf_all().wait_send()
    xf_all().wait_send()

    weight_load.wait()

    def update(block, delta):
        place = pl.ds(pl.multiple_of(block * 1024, 1024), 1024)
        value = weight[:, place].astype(F32) - step_rate * delta.astype(F32)
        weight_out[:, place] = value.astype(BF16)

    update(z, d_send[0])
    for i in range(1, 8):
        d_copy(i).wait_recv()
        update(along_z(RING[i]), d_recv[i - 1])
    for i in range(1, 8):
        d_copy(i).wait_send()


def store(weight, first, second, weight_out, first_out, second_out, sem):
    copies = [
        pltpu.make_async_copy(source, target, sem.at[i])
        for i, (source, target) in enumerate(((weight, weight_out), (first, first_out), (second, second_out)))
    ]
    for copy in copies:
        copy.start()
    for copy in copies:
        copy.wait()


def body(activations, cotangent, basis, weight, first_moment, second_moment):
    vmem, dma = pltpu.VMEM, pltpu.SemaphoreType.DMA
    results = pl.pallas_call(
        kernel,
        out_shape=(vmem((16, 8192), BF16), vmem((16, 1024), F32), vmem((16, 1024), F32)),
        in_specs=[pl.BlockSpec(memory_space=pltpu.HBM)] * 6,
        out_specs=(pl.BlockSpec(memory_space=pltpu.VMEM),) * 3,
        scratch_shapes=[
            vmem((512, 1024), BF16),
            vmem((512, 1024), BF16),
            vmem((CHUNKS, 1024, WIDTH), BF16),
            vmem((16, 8192), BF16),
            vmem((16, 1024), F32),
            vmem((16, 1024), F32),
            vmem((CHUNKS, 8, 64, WIDTH), F32),
            vmem((CHUNKS, 7, 64, WIDTH), BF16),
            vmem((CHUNKS, 7, 64, WIDTH), BF16),
            vmem((CHUNKS, 8, 64, WIDTH), BF16),
            vmem((2, 4, 8, 16, 512), BF16),
            vmem((CHUNKS, 4, 8, 16, WIDTH), F32),
            vmem((CHUNKS, 4, 8, 16, WIDTH), BF16),
            vmem((CHUNKS, 4, 8, 16, WIDTH), BF16),
            vmem((CHUNKS, 3, 8, 16, WIDTH), BF16),
            vmem((CHUNKS, 3, 8, 16, WIDTH), BF16),
            vmem((CHUNKS, 8, 16, WIDTH), F32),
            vmem((CHUNKS, 7, 16, WIDTH), BF16),
            vmem((CHUNKS, 7, 16, WIDTH), BF16),
            vmem((7, 4, 16, WIDTH), BF16),
            vmem((7, 4, 16, WIDTH), BF16),
            vmem((4, 16, WIDTH), F32),
            vmem((3, 16, WIDTH), BF16),
            vmem((3, 16, WIDTH), BF16),
            vmem((CHUNKS, 8, 16, WIDTH), BF16),
            vmem((128, 1024), F32),
            vmem((8, 16, 1024), BF16),
            vmem((7, 16, 1024), BF16),
            dma((5 + CHUNKS,)),
            dma((CHUNKS, 7)),
            dma((CHUNKS, 7)),
            dma((CHUNKS, 7)),
            dma((CHUNKS, 7)),
            dma((CHUNKS,)),
            dma((CHUNKS,)),
            dma((CHUNKS,)),
            dma((CHUNKS,)),
            dma((CHUNKS,)),
            dma((CHUNKS,)),
            dma((CHUNKS,)),
            dma((CHUNKS, 2)),
            dma((7,)),
            dma((7,)),
            dma((4,)),
            pltpu.SemaphoreType.REGULAR,
            pltpu.SemaphoreType.REGULAR,
        ],
        compiler_params=pltpu.CompilerParams(
            collective_id=1, has_side_effects=True, vmem_limit_bytes=60 * 2**20
        ),
        name="galore_step",
    )(activations, cotangent, basis, weight, first_moment, second_moment)
    return pl.pallas_call(
        store,
        out_shape=tuple(jax.ShapeDtypeStruct(r.shape, r.dtype) for r in results),
        in_specs=[pl.BlockSpec(memory_space=pltpu.VMEM)] * 3,
        out_specs=(pl.BlockSpec(memory_space=pltpu.HBM),) * 3,
        scratch_shapes=[dma((3,))],
        compiler_params=pltpu.CompilerParams(vmem_limit_bytes=2 * 2**20),
        name="store_results",
    )(*results)


def solution(mesh):
    rows = P(("mp", "dp"), None)
    return jax.shard_map(
        body,
        mesh=mesh,
        in_specs=(P("dp", "mp"), P("dp", "mp"), P("mp", None), rows, rows, rows),
        out_specs=(rows, rows, rows),
        check_vma=False,
    )
```
